256 devices in a mesh: expert: 32 (over z, x), mp: 8 (over y, core).
Axes of the slice: x: 4, y: 4, z: 8, core: 2. Of those that a mesh axis runs over, the one named last changes fastest.
Arguments:
- base_weights: bfloat16 [32, 7168, 1024], P('expert', 'mp'), may hold values from -6 to 6
- deltas: bfloat16 [3, 32, 7168, 1024], P(None, 'expert', 'mp'), may hold values from -1.6 to 1.6
- keep_flags: int32 [3, 32, 896, 8], P(None, 'expert', 'mp'), may hold values 0 or 1
- serve_order: int32 [32], replicated, may hold values from 0 to 31, each once
Outputs:
- served_weights: bfloat16 [32, 1024, 7168], P(None, 'expert', 'mp')
- checksums: float32 [32], P('expert')
- largest_change: float32 [32], P('expert')
The draws below stay inside these ranges and needn't reach their ends.
Inputs may be any that keep to these rules, and one draw needn't show every extreme that they name: `serve_order`: each expert appears in exactly one slot.
All inputs are finite; a program needn't handle non-finite values. No bound on the sum of `keep_flags` on one device may be relied on, other than what follows from the above.
Results may differ from the reference program's by a relative error of at most 0.008.
Values may be sent and summed in bfloat16 or wider, within the bound.
No kernel may reach another device: no remote copies, remote signals or barrier semaphores. Data moves between devices by JAX's collectives and lax.ppermute only.
A program may use at most 64 MiB of HBM per device.

```python
import math
import jax
import jax.numpy as jnp
from jax import lax

D = 7168
F = 1024
CKPTS = 3
EXPERTS = 32


def draw_deltas(key, part):
    folded = jax.random.fold_in(key, 11)
    key_scale, key_value = jax.random.split(folded)
    key_band = jax.random.fold_in(folded, 23)
    scales = jnp.exp(jax.random.uniform(key_scale, (1, EXPERTS, 1, 1, 1), jnp.float32, math.log(0.03), math.log(0.13)))
    bands = jnp.exp(jax.random.uniform(key_band, (1, EXPERTS, 8, 1, 1), jnp.float32, math.log(0.3), math.log(3.0)))
    values = jnp.clip(jax.random.normal(key_value, (CKPTS, EXPERTS, 8, D // 8, F), jnp.float32), -4.0, 4.0)
    shaped = (values * scales * bands).reshape(CKPTS, EXPERTS, D, F)
    return shaped.astype(jnp.bfloat16)


def set_ends(entries, own_key, smallest, high):
    longest = entries.shape.index(max(entries.shape))
    spots = []
    for shift in (0, 1):
        where = [jax.random.randint(jax.random.fold_in(own_key, axis), (), 0, length) for axis, length in enumerate(entries.shape)]
        where[longest] = (where[longest] + shift) % entries.shape[longest]
        spots.append(tuple(where))
    return entries.at[spots[0]].set(smallest).at[spots[1]].set(high)


def shard_levels(own_key, dims, shards, smallest, high):
    def one(axis_at, parts):
        draws = jax.random.uniform(jax.random.fold_in(jax.random.fold_in(own_key, 6), axis_at), (parts,), jnp.float32, smallest / len(shards), high / len(shards))
        return jnp.repeat(jnp.exp(draws), dims[axis_at] // parts).reshape((-1,) + (1,) * (len(dims) - axis_at - 1))

    loudness = one(*shards[0])
    for cut in shards[1:]:
        loudness = loudness * one(*cut)
    return loudness


def noise(stream_key, shape, spread, most, cuts=(), kind=jnp.bfloat16):
    factor_of = shard_levels(stream_key, shape, cuts, -0.22, 0.18) if cuts else 1.0
    drawn = jax.random.normal(stream_key, shape, jnp.float32) * spread * factor_of
    return jnp.minimum(jnp.maximum(drawn, -most), most).astype(kind)


def setup_inputs(seed: int = 0) -> dict:
    keys = jax.random.split(jax.random.key(seed), 5)
    base_weights = noise(keys[0], (EXPERTS, D, F), 1.0, 6.0, ((0, 32), (1, 8)))
    deltas = draw_deltas(jax.random.fold_in(keys[4], 71), 0)
    keep_flags = set_ends((jax.random.randint(keys[2], (CKPTS, EXPERTS, D // 8, F // 128), 0, 3) < 1).astype(jnp.int32), jax.random.fold_in(keys[2], 1), 0, 1)
    serve_order = jax.random.permutation(keys[3], EXPERTS).astype(jnp.int32)
    return dict(base_weights=base_weights, deltas=deltas, keep_flags=keep_flags, serve_order=serve_order)


def merge_block(base_rows, delta_rows, keep_rows):
    experts_here, row_count, columns = base_rows.shape
    expanded = keep_rows.astype(jnp.float32)[:, :, :, None, :, None]
    trimmed = delta_rows.astype(jnp.float32).reshape(3, experts_here, row_count // 8, 8, columns // 128, 128) * expanded
    trimmed = trimmed.reshape(3, experts_here, row_count, columns)
    elected = jnp.sign(trimmed[0] + trimmed[1] + trimmed[2])
    agreeing = (trimmed * elected > 0).astype(jnp.float32)
    voters = lax.optimization_barrier(jnp.sum(agreeing, axis=0))
    update = lax.optimization_barrier(jnp.sum(trimmed * agreeing, axis=0)) / jnp.maximum(voters, 1.0)
    merged = (base_rows.astype(jnp.float32) + update).astype(jnp.bfloat16)
    return (merged, update)

def reference(base_weights, deltas, keep_flags, serve_order):

    def per_expert(bundle):
        base_one, delta_one, keep_one = bundle
        merged, update = merge_block(base_one[None], delta_one[:, None], keep_one[:, None])
        checksum = jnp.sum(merged.astype(jnp.float32)) / math.sqrt(D * F)
        largest = jnp.max(jnp.abs(update))
        return (jnp.swapaxes(merged[0], 0, 1), checksum, largest)
    serving, checks, largest = lax.map(per_expert, (base_weights, jnp.moveaxis(deltas, 1, 0), jnp.moveaxis(keep_flags, 1, 0)))
    return (jnp.take(serving, serve_order, axis=0), checks, largest)
```

```python
import functools
import math

import jax
import jax.numpy as jnp
from jax import lax
from jax.experimental import pallas as pl
from jax.experimental.pallas import tpu as pltpu
from jax.sharding import PartitionSpec as P

D = 7168
F = 1024
LANES = 128


def merge_kernel(keep_ref, base_ref, delta_ref, out_ref, sums_ref, largest_ref, spread_ref):
    step = pl.program_id(0)
    rows, columns = base_ref.shape[1:]
    blocks = rows // 8
    flags = keep_ref[:, 0].astype(jnp.float32).reshape(3 * blocks, columns // LANES)
    lane_block = lax.broadcasted_iota(jnp.int32, (columns // LANES, columns), 1) // LANES
    own_block = lax.broadcasted_iota(jnp.int32, (columns // LANES, columns), 0)
    expand = (lane_block == own_block).astype(jnp.float32)
    spread_ref[...] = jnp.dot(flags, expand, preferred_element_type=jnp.float32)

    @pl.when(step == 0)
    def _():
        sums_ref[...] = jnp.zeros_like(sums_ref)
        largest_ref[...] = jnp.zeros_like(largest_ref)

    total = jnp.zeros((8, LANES), jnp.float32)
    largest = jnp.zeros((8, LANES), jnp.float32)
    for c in range(columns // LANES):
        cols = pl.ds(c * LANES, LANES)
        t = []
        for k in range(3):
            d = delta_ref[k, 0, :, cols].astype(jnp.float32).reshape(blocks, 8, LANES)
            kept = spread_ref[pl.ds(k * blocks, blocks), cols]
            t.append(d * kept[:, None, :])
        s = t[0] + t[1] + t[2]
        sign = jnp.where(s > 0, 1.0, jnp.where(s < 0, -1.0, 0.0))
        u = [x * sign for x in t]
        chosen = jnp.maximum(u[0], 0.0) + jnp.maximum(u[1], 0.0) + jnp.maximum(u[2], 0.0)
        voters = sum(jnp.where(x > 0, 1.0, 0.0) for x in u)
        share = jnp.where(voters > 2.5, 1.0 / 3.0, jnp.where(voters > 1.5, 0.5, 1.0))
        size = chosen * share
        update = (size * sign).reshape(rows, LANES)
        merged = (base_ref[0, :, cols].astype(jnp.float32) + update).astype(jnp.bfloat16)
        total = total + merged.astype(jnp.float32).reshape(blocks, 8, LANES).sum(axis=0)
        largest = jnp.maximum(largest, size.max(axis=0))
        turned = merged.T
        out_ref[pl.ds(c * 4, 4)] = turned.reshape(4, LANES // 4, rows)
    sums_ref[...] += total
    largest_ref[...] = jnp.maximum(largest_ref[...], largest)


def merge(base_weights, deltas, keep_flags):
    _, rows, columns = base_weights.shape
    step = LANES
    n = 32
    return pl.pallas_call(
        merge_kernel,
        grid=(rows // step,),
        in_specs=[
            pl.BlockSpec((3, 1, step // 8, columns // LANES), lambda i: (0, 0, i, 0)),
            pl.BlockSpec((1, step, columns), lambda i: (0, i, 0)),
            pl.BlockSpec((3, 1, step, columns), lambda i: (0, 0, i, 0)),
        ],
        out_specs=[
            pl.BlockSpec((n, columns // n, step), lambda i: (0, 0, i)),
            pl.BlockSpec((8, LANES), lambda i: (0, 0)),
            pl.BlockSpec((8, LANES), lambda i: (0, 0)),
        ],
        out_shape=[
            jax.ShapeDtypeStruct((n, columns // n, rows), jnp.bfloat16),
            jax.ShapeDtypeStruct((8, LANES), jnp.float32),
            jax.ShapeDtypeStruct((8, LANES), jnp.float32),
        ],
        scratch_shapes=[pltpu.VMEM((3 * step // 8, columns), jnp.float32)],
        compiler_params=pltpu.CompilerParams(vmem_limit_bytes=16 * 2**20),
    )(keep_flags, base_weights, deltas)


def place_kernel(order_ref, in_ref, out_ref, sems):
    n = out_ref.shape[0]
    for s in range(n):
        pltpu.make_async_copy(in_ref.at[order_ref[s]], out_ref.at[s], sems.at[s]).start()
    for s in range(n):
        pltpu.make_async_copy(in_ref.at[order_ref[s]], out_ref.at[s], sems.at[s]).wait()


def place(arranged, serve_order):
    n = arranged.shape[0]
    return pl.pallas_call(
        place_kernel,
        in_specs=[
            pl.BlockSpec(memory_space=pltpu.SMEM),
            pl.BlockSpec(memory_space=pl.ANY),
        ],
        out_specs=pl.BlockSpec(memory_space=pl.ANY),
        out_shape=jax.ShapeDtypeStruct(arranged.shape, arranged.dtype),
        scratch_shapes=[pltpu.SemaphoreType.DMA((n,))],
        compiler_params=pltpu.CompilerParams(vmem_limit_bytes=4 * 2**20),
    )(serve_order, arranged)


def on_device(base_weights, deltas, keep_flags, serve_order):
    merged, sums, largest = merge(base_weights, deltas, keep_flags)
    arranged = lax.all_to_all(merged, "expert", split_axis=0, concat_axis=0, tiled=True)
    total_here = jnp.sum(sums).reshape(1)
    largest_here = jnp.max(largest).reshape(1)
    both = lax.all_gather(jnp.concatenate([total_here, largest_here]), "mp")
    serving = place(arranged, serve_order)
    return (serving, both[:, 0].sum(0)[None] / math.sqrt(D * F), both[:, 1].max(0)[None])


def solution(mesh):
    in_specs = (
        P("expert", "mp", None),
        P(None, "expert", "mp", None),
        P(None, "expert", "mp", None),
        P(),
    )
    out_specs = (P(None, "expert", "mp"), P("expert"), P("expert"))
    return jax.shard_map(
        on_device, mesh=mesh, in_specs=in_specs, out_specs=out_specs, check_vma=False
    )
```

```python
import math

import jax
import jax.numpy as jnp
from jax import lax
from jax.experimental import pallas as pl
from jax.experimental.pallas import tpu as pltpu
from jax.sharding import PartitionSpec as P

D = 7168
F = 1024
LANES = 128
STEP = 128
ORDER = [
    19, 28, 1, 17, 12, 22, 16, 30, 15, 23, 11, 24, 6, 9, 31, 14,
    25, 4, 26, 2, 27, 13, 0, 5, 18, 7, 3, 29, 20, 21, 8, 10,
]
PLACE_OF = [ORDER.index(e) for e in range(32)]
VMEM_BYTES = 60 * 2**20


def spread_flags(flags, columns):
    lane_block = lax.broadcasted_iota(jnp.int32, (flags.shape[0], columns), 1) // LANES
    own_block = lax.broadcasted_iota(jnp.int32, (flags.shape[0], columns), 0)
    expand = (lane_block == own_block).astype(jnp.float32)
    return lax.dot_general(
        flags.astype(jnp.float32),
        expand,
        (((0,), (0,)), ((), ())),
        preferred_element_type=jnp.float32,
    )


def voted_update(t):
    s = t[0] + t[1] + t[2]
    sign = jnp.where(s > 0, 1.0, jnp.where(s < 0, -1.0, 0.0))
    a, b, c = (x * sign for x in t)
    low, high = jnp.minimum(a, b), jnp.maximum(a, b)
    most, least = jnp.maximum(high, c), jnp.minimum(low, c)
    middle = jnp.maximum(low, jnp.minimum(high, c))
    few = jnp.where(middle > 0, (most + middle) * 0.5, most) * sign
    return jnp.where(least > 0, s * (1.0 / 3.0), few)


def trimmed_tile(delta_at, flags_at):
    out = []
    for k in range(3):
        d = delta_at(k).astype(jnp.float32)
        rows = d.shape[0]
        out.append(d.reshape(rows // 8, 8, LANES) * flags_at(k)[:, None, :])
    return out


def merge_kernel(
    keep_hbm, base_hbm, delta_hbm, out_hbm, d_buf, b_buf, o_buf, k_buf, spread_ref, in_sems, out_sems, k_sem
):
    rows_all, columns = b_buf.shape
    n = rows_all // STEP
    blocks = STEP // 8

    def rows_of(i):
        return pl.ds(pl.multiple_of(i * STEP, STEP), STEP)

    def delta_copy(i):
        return pltpu.make_async_copy(delta_hbm.at[:, 0, rows_of(i)], d_buf.at[:, rows_of(i)], in_sems.at[i, 0])

    def base_copy(i):
        return pltpu.make_async_copy(base_hbm.at[0, rows_of(i)], b_buf.at[rows_of(i)], in_sems.at[i, 1])

    def out_copy(i):
        return pltpu.make_async_copy(o_buf.at[i], out_hbm.at[:, :, rows_of(i)], out_sems.at[i])

    keep_copy = pltpu.make_async_copy(keep_hbm, k_buf, k_sem)
    def fetch(i):
        delta_copy(i).start()
        base_copy(i).start()

    keep_copy.start()
    fetch(0)
    keep_copy.wait()
    for k in range(3):
        spread_ref[k] = spread_flags(k_buf[k, 0], columns)
    fetch(1)

    def chunk(i, carry):
        delta_copy(i).wait()
        base_copy(i).wait()

        @pl.when(i + 2 < n)
        def _():
            fetch(i + 2)

        flag_rows = pl.ds(pl.multiple_of(i * blocks, blocks), blocks)
        for c in range(columns // LANES):
            cols = pl.ds(c * LANES, LANES)
            t = trimmed_tile(lambda k: d_buf[k, rows_of(i), cols], lambda k: spread_ref[k, flag_rows, cols])
            base = b_buf[rows_of(i), cols].astype(jnp.float32).reshape(blocks, 8, LANES)
            merged = (base + voted_update(t)).reshape(STEP, LANES).astype(jnp.bfloat16)
            turned = merged.T.reshape(4, LANES // 4, STEP)
            for j in range(4):
                o_buf[i, PLACE_OF[c * 4 + j]] = turned[j]
        out_copy(i).start()
        return carry

    lax.fori_loop(0, n, chunk, 0)
    for i in range(n):
        out_copy(i).wait()


def merge(base_weights, deltas, keep_turned):
    _, rows, columns = base_weights.shape
    n = rows // STEP
    slots = len(ORDER)
    return pl.pallas_call(
        merge_kernel,
        in_specs=[pl.BlockSpec(memory_space=pl.ANY)] * 3,
        out_specs=pl.BlockSpec(memory_space=pl.ANY),
        out_shape=jax.ShapeDtypeStruct((slots, columns // slots, rows), jnp.bfloat16),
        scratch_shapes=[
            pltpu.VMEM((3, rows, columns), jnp.bfloat16),
            pltpu.VMEM((rows, columns), jnp.bfloat16),
            pltpu.VMEM((n, slots, columns // slots, STEP), jnp.bfloat16),
            pltpu.VMEM(keep_turned.shape, jnp.int32),
            pltpu.VMEM((3, rows // 8, columns), jnp.float32),
            pltpu.SemaphoreType.DMA((n, 2)),
            pltpu.SemaphoreType.DMA((n,)),
            pltpu.SemaphoreType.DMA,
        ],
        compiler_params=pltpu.CompilerParams(vmem_limit_bytes=VMEM_BYTES),
    )(keep_turned, base_weights, deltas)


def figures_kernel(keep_ref, delta_ref, merged_ref, sums_ref, largest_ref, spread_ref):
    step = pl.program_id(0)
    columns = delta_ref.shape[3]
    blocks = STEP // 8

    @pl.when(step == 0)
    def _():
        sums_ref[...] = jnp.zeros_like(sums_ref)
        largest_ref[...] = jnp.zeros_like(largest_ref)
        for k in range(3):
            spread_ref[k] = spread_flags(keep_ref[k, 0], columns)

    flag_rows = pl.ds(pl.multiple_of(step * blocks, blocks), blocks)
    largest = largest_ref[...]
    for c in range(columns // LANES):
        cols = pl.ds(c * LANES, LANES)
        t = trimmed_tile(lambda k: delta_ref[k, 0, :, cols], lambda k: spread_ref[k, flag_rows, cols])
        largest = jnp.maximum(largest, jnp.abs(voted_update(t)).max(axis=0))
    largest_ref[...] = largest
    total = sums_ref[...]
    for s in range(merged_ref.shape[0]):
        m = merged_ref[s].astype(jnp.float32)
        total = total + m.reshape(m.shape[0] // 8, 8, LANES).sum(axis=0)
    sums_ref[...] = total


def figures(keep_turned, deltas, merged):
    _, _, rows, columns = deltas.shape
    slots, height, _ = merged.shape
    return pl.pallas_call(
        figures_kernel,
        grid=(rows // STEP,),
        in_specs=[
            pl.BlockSpec(keep_turned.shape, lambda i: (0, 0, 0, 0)),
            pl.BlockSpec((3, 1, STEP, columns), lambda i: (0, 0, i, 0)),
            pl.BlockSpec((slots, height, STEP), lambda i: (0, 0, i)),
        ],
        out_specs=[pl.BlockSpec((8, LANES), lambda i: (0, 0))] * 2,
        out_shape=[jax.ShapeDtypeStruct((8, LANES), jnp.float32)] * 2,
        scratch_shapes=[pltpu.VMEM((3, rows // 8, columns), jnp.float32)],
        compiler_params=pltpu.CompilerParams(vmem_limit_bytes=VMEM_BYTES),
    )(keep_turned, deltas, merged)


def place_kernel(order_ref, place_ref, in_ref, out_ref, sems):
    def copy(s):
        return pltpu.make_async_copy(in_ref.at[place_ref[order_ref[s]]], out_ref.at[s], sems.at[s])

    for s in range(out_ref.shape[0]):
        copy(s).start()
    for s in range(out_ref.shape[0]):
        copy(s).wait()


def place(arranged, serve_order):
    n = arranged.shape[0]
    return pl.pallas_call(
        place_kernel,
        in_specs=[
            pl.BlockSpec(memory_space=pltpu.SMEM),
            pl.BlockSpec(memory_space=pltpu.SMEM),
            pl.BlockSpec(memory_space=pl.ANY),
        ],
        out_specs=pl.BlockSpec(memory_space=pl.ANY),
        out_shape=jax.ShapeDtypeStruct(arranged.shape, arranged.dtype),
        scratch_shapes=[pltpu.SemaphoreType.DMA((n,))],
        compiler_params=pltpu.CompilerParams(vmem_limit_bytes=4 * 2**20),
    )(serve_order, jnp.array(PLACE_OF, jnp.int32), arranged)


def on_device(base_weights, deltas, keep_flags, serve_order):
    keep_turned = jnp.swapaxes(keep_flags, 2, 3)
    merged = merge(base_weights, deltas, keep_turned)
    arranged = lax.all_to_all(
        merged, "expert", split_axis=0, concat_axis=0, tiled=True, axis_index_groups=[ORDER]
    )
    sums, largest = figures(keep_turned, deltas, merged)
    here = jnp.stack([jnp.sum(sums), jnp.max(largest)])
    both = lax.all_gather(here, "mp")
    serving = place(arranged, serve_order)
    return (serving, both[:, 0].sum(0)[None] / math.sqrt(D * F), both[:, 1].max(0)[None])


def solution(mesh):
    in_specs = (
        P("expert", "mp", None),
        P(None, "expert", "mp", None),
        P(None, "expert", "mp", None),
        P(),
    )
    out_specs = (P(None, "expert", "mp"), P("expert"), P("expert"))
    return jax.shard_map(
        on_device, mesh=mesh, in_specs=in_specs, out_specs=out_specs, check_vma=False
    )
```

```python
import math

import jax
import jax.numpy as jnp
from jax import lax
from jax.experimental import pallas as pl
from jax.experimental.pallas import tpu as pltpu
from jax.sharding import PartitionSpec as P

D = 7168
F = 1024
LANES = 128
STEP = 128
ORDER = [
    19, 28, 1, 17, 12, 22, 16, 30, 15, 23, 11, 24, 6, 9, 31, 14,
    25, 4, 26, 2, 27, 13, 0, 5, 18, 7, 3, 29, 20, 21, 8, 10,
]
PLACE_OF = [ORDER.index(e) for e in range(32)]
VMEM_BYTES = 60 * 2**20


def spread_flags(flags, columns):
    lane_block = lax.broadcasted_iota(jnp.int32, (flags.shape[0], columns), 1) // LANES
    own_block = lax.broadcasted_iota(jnp.int32, (flags.shape[0], columns), 0)
    expand = (lane_block == own_block).astype(jnp.float32)
    return lax.dot_general(
        flags.astype(jnp.float32),
        expand,
        (((0,), (0,)), ((), ())),
        preferred_element_type=jnp.float32,
    )


def voted_update(t):
    s = t[0] + t[1] + t[2]
    sign = jnp.where(s > 0, 1.0, jnp.where(s < 0, -1.0, 0.0))
    a, b, c = (x * sign for x in t)
    low, high = jnp.minimum(a, b), jnp.maximum(a, b)
    most, least = jnp.maximum(high, c), jnp.minimum(low, c)
    middle = jnp.maximum(low, jnp.minimum(high, c))
    few = jnp.where(middle > 0, (most + middle) * 0.5, most) * sign
    return jnp.where(least > 0, s * (1.0 / 3.0), few)


def trimmed_tile(delta_at, flags_at):
    out = []
    for k in range(3):
        d = delta_at(k).astype(jnp.float32)
        rows = d.shape[0]
        out.append(d.reshape(rows // 8, 8, LANES) * flags_at(k)[:, None, :])
    return out


def merge_kernel(
    keep_hbm, base_hbm, delta_hbm, out_hbm, d_buf, b_buf, o_buf, k_buf, spread_ref, in_sems, out_sems, k_sem
):
    rows_all, columns = b_buf.shape
    n = rows_all // STEP
    blocks = STEP // 8

    def rows_of(i):
        return pl.ds(pl.multiple_of(i * STEP, STEP), STEP)

    def delta_copy(i):
        return pltpu.make_async_copy(delta_hbm.at[:, 0, rows_of(i)], d_buf.at[:, rows_of(i)], in_sems.at[i, 0])

    def base_copy(i):
        return pltpu.make_async_copy(base_hbm.at[0, rows_of(i)], b_buf.at[rows_of(i)], in_sems.at[i, 1])

    def out_copy(i):
        return pltpu.make_async_copy(o_buf.at[i], out_hbm.at[:, :, rows_of(i)], out_sems.at[i])

    keep_copy = pltpu.make_async_copy(keep_hbm, k_buf, k_sem)
    def fetch(i):
        delta_copy(i).start()
        base_copy(i).start()

    keep_copy.start()
    fetch(0)
    keep_copy.wait()
    for k in range(3):
        spread_ref[k] = spread_flags(k_buf[k, 0], columns)
    for i in range(1, n):
        fetch(i)

    def chunk(i, carry):
        delta_copy(i).wait()
        base_copy(i).wait()
        flag_rows = pl.ds(pl.multiple_of(i * blocks, blocks), blocks)
        for c in range(columns // LANES):
            cols = pl.ds(c * LANES, LANES)
            t = trimmed_tile(lambda k: d_buf[k, rows_of(i), cols], lambda k: spread_ref[k, flag_rows, cols])
            base = b_buf[rows_of(i), cols].astype(jnp.float32).reshape(blocks, 8, LANES)
            merged = (base + voted_update(t)).reshape(STEP, LANES).astype(jnp.bfloat16)
            turned = merged.T.reshape(4, LANES // 4, STEP)
            for j in range(4):
                o_buf[i, PLACE_OF[c * 4 + j]] = turned[j]
        out_copy(i).start()
        return carry

    lax.fori_loop(0, n, chunk, 0)
    for i in range(n):
        out_copy(i).wait()


def merge(base_weights, deltas, keep_turned):
    _, rows, columns = base_weights.shape
    n = rows // STEP
    slots = len(ORDER)
    return pl.pallas_call(
        merge_kernel,
        in_specs=[pl.BlockSpec(memory_space=pl.ANY)] * 3,
        out_specs=pl.BlockSpec(memory_space=pl.ANY),
        out_shape=jax.ShapeDtypeStruct((slots, columns // slots, rows), jnp.bfloat16),
        scratch_shapes=[
            pltpu.VMEM((3, rows, columns), jnp.bfloat16),
            pltpu.VMEM((rows, columns), jnp.bfloat16),
            pltpu.VMEM((n, slots, columns // slots, STEP), jnp.bfloat16),
            pltpu.VMEM(keep_turned.shape, jnp.int32),
            pltpu.VMEM((3, rows // 8, columns), jnp.float32),
            pltpu.SemaphoreType.DMA((n, 2)),
            pltpu.SemaphoreType.DMA((n,)),
            pltpu.SemaphoreType.DMA,
        ],
        compiler_params=pltpu.CompilerParams(vmem_limit_bytes=VMEM_BYTES),
    )(keep_turned, base_weights, deltas)


def figures_kernel(keep_ref, delta_ref, merged_ref, sums_ref, largest_ref, spread_ref):
    step = pl.program_id(0)
    columns = delta_ref.shape[3]
    blocks = STEP // 8

    @pl.when(step == 0)
    def _():
        sums_ref[...] = jnp.zeros_like(sums_ref)
        largest_ref[...] = jnp.zeros_like(largest_ref)
        for k in range(3):
            spread_ref[k] = spread_flags(keep_ref[k, 0], columns)

    flag_rows = pl.ds(pl.multiple_of(step * blocks, blocks), blocks)
    largest = largest_ref[...]
    for c in range(columns // LANES):
        cols = pl.ds(c * LANES, LANES)
        t = trimmed_tile(lambda k: delta_ref[k, 0, :, cols], lambda k: spread_ref[k, flag_rows, cols])
        largest = jnp.maximum(largest, jnp.abs(voted_update(t)).max(axis=0))
    largest_ref[...] = largest
    total = sums_ref[...]
    for s in range(merged_ref.shape[0]):
        m = merged_ref[s].astype(jnp.float32)
        total = total + m.reshape(m.shape[0] // 8, 8, LANES).sum(axis=0)
    sums_ref[...] = total


def figures(keep_turned, deltas, merged):
    _, _, rows, columns = deltas.shape
    slots, height, _ = merged.shape
    return pl.pallas_call(
        figures_kernel,
        grid=(rows // STEP,),
        in_specs=[
            pl.BlockSpec(keep_turned.shape, lambda i: (0, 0, 0, 0)),
            pl.BlockSpec((3, 1, STEP, columns), lambda i: (0, 0, i, 0)),
            pl.BlockSpec((slots, height, STEP), lambda i: (0, 0, i)),
        ],
        out_specs=[pl.BlockSpec((8, LANES), lambda i: (0, 0))] * 2,
        out_shape=[jax.ShapeDtypeStruct((8, LANES), jnp.float32)] * 2,
        scratch_shapes=[pltpu.VMEM((3, rows // 8, columns), jnp.float32)],
        compiler_params=pltpu.CompilerParams(vmem_limit_bytes=VMEM_BYTES),
    )(keep_turned, deltas, merged)


def totals_kernel(both_ref, total_ref, largest_ref):
    total_ref[0] = jnp.sum(both_ref[:, 0:1]) * (1.0 / math.sqrt(D * F))
    largest_ref[0] = jnp.max(both_ref[:, 1:2])


def totals(both):
    one = jax.ShapeDtypeStruct((1,), jnp.float32)
    return pl.pallas_call(
        totals_kernel,
        in_specs=[pl.BlockSpec(memory_space=pltpu.VMEM)],
        out_specs=[pl.BlockSpec(memory_space=pltpu.SMEM)] * 2,
        out_shape=[one, one],
    )(both)


def place_kernel(order_ref, place_ref, in_ref, out_ref, sems):
    def copy(s):
        return pltpu.make_async_copy(in_ref.at[place_ref[order_ref[s]]], out_ref.at[s], sems.at[s])

    for s in range(out_ref.shape[0]):
        copy(s).start()
    for s in range(out_ref.shape[0]):
        copy(s).wait()


def place(arranged, serve_order):
    n = arranged.shape[0]
    return pl.pallas_call(
        place_kernel,
        in_specs=[
            pl.BlockSpec(memory_space=pltpu.SMEM),
            pl.BlockSpec(memory_space=pltpu.SMEM),
            pl.BlockSpec(memory_space=pl.ANY),
        ],
        out_specs=pl.BlockSpec(memory_space=pl.ANY),
        out_shape=jax.ShapeDtypeStruct(arranged.shape, arranged.dtype),
        scratch_shapes=[pltpu.SemaphoreType.DMA((n,))],
        compiler_params=pltpu.CompilerParams(vmem_limit_bytes=4 * 2**20),
    )(serve_order, jnp.array(PLACE_OF, jnp.int32), arranged)


def on_device(base_weights, deltas, keep_flags, serve_order):
    keep_turned = jnp.swapaxes(keep_flags, 2, 3)
    merged = merge(base_weights, deltas, keep_turned)
    arranged = lax.all_to_all(
        merged, "expert", split_axis=0, concat_axis=0, tiled=True, axis_index_groups=[ORDER]
    )
    sums, largest = figures(keep_turned, deltas, merged)
    here = jnp.stack([jnp.sum(sums), jnp.max(largest)])
    both = lax.all_gather(here, "mp")
    total, largest = totals(both)
    serving = place(arranged, serve_order)
    return (serving, total, largest)


def solution(mesh):
    in_specs = (
        P("expert", "mp", None),
        P(None, "expert", "mp", None),
        P(None, "expert", "mp", None),
        P(),
    )
    out_specs = (P(None, "expert", "mp"), P("expert"), P("expert"))
    return jax.shard_map(
        on_device, mesh=mesh, in_specs=in_specs, out_specs=out_specs, check_vma=False
    )
```

```python
import math

import jax
import jax.numpy as jnp
from jax import lax
from jax.experimental import pallas as pl
from jax.experimental.pallas import tpu as pltpu
from jax.sharding import PartitionSpec as P

D = 7168
F = 1024
LANES = 128
STEP = 128
ORDER = [
    19, 28, 1, 17, 12, 22, 16, 30, 15, 6, 9, 31, 14, 25, 4, 26,
    2, 27, 13, 0, 5, 23, 11, 24, 18, 7, 3, 29, 20, 21, 8, 10,
]
PLACE_OF = [ORDER.index(e) for e in range(32)]
VMEM_BYTES = 60 * 2**20


def spread_flags(flags_ref, spread_ref, columns):
    for k in range(3):
        spread = spread_over_lanes(flags_ref[k, 0], columns)
        for c in range(columns // LANES):
            spread_ref[k, c, pl.ds(0, spread.shape[0])] = spread[:, c * LANES : (c + 1) * LANES]


def spread_scratch(rows, columns):
    return pltpu.VMEM((3, columns // LANES, rows // 8 + 8, LANES), jnp.float32)


def spread_over_lanes(flags, columns):
    lane_block = lax.broadcasted_iota(jnp.int32, (flags.shape[0], columns), 1) // LANES
    own_block = lax.broadcasted_iota(jnp.int32, (flags.shape[0], columns), 0)
    expand = (lane_block == own_block).astype(jnp.float32)
    return lax.dot_general(
        flags.astype(jnp.float32),
        expand,
        (((0,), (0,)), ((), ())),
        preferred_element_type=jnp.float32,
    )


def voted_update(t):
    s = t[0] + t[1] + t[2]
    sign = jnp.where(s > 0, 1.0, jnp.where(s < 0, -1.0, 0.0))
    a, b, c = (x * sign for x in t)
    low, high = jnp.minimum(a, b), jnp.maximum(a, b)
    most, least = jnp.maximum(high, c), jnp.minimum(low, c)
    middle = jnp.maximum(low, jnp.minimum(high, c))
    few = jnp.where(middle > 0, (most + middle) * 0.5, most) * sign
    return jnp.where(least > 0, s * (1.0 / 3.0), few)


def trimmed_tile(delta_at, spread_ref, column_block, first_block):
    out = []
    for k in range(3):
        d = delta_at(k).astype(jnp.float32)
        blocks = d.shape[0] // 8
        d = d.reshape(blocks, 8, LANES)
        kept = [spread_ref[k, column_block, pl.ds(first_block + r, 8, stride=0)] for r in range(blocks)]
        out.append(jnp.stack([d[r] * kept[r] for r in range(blocks)]))
    return out


def merge_kernel(
    keep_hbm, base_hbm, delta_hbm, out_hbm, d_buf, b_buf, o_buf, k_buf, spread_ref, in_sems, out_sems, k_sem
):
    rows_all, columns = b_buf.shape
    n = rows_all // STEP
    blocks = STEP // 8

    def rows_of(i):
        return pl.ds(pl.multiple_of(i * STEP, STEP), STEP)

    def delta_copy(i):
        return pltpu.make_async_copy(delta_hbm.at[:, 0, rows_of(i)], d_buf.at[:, rows_of(i)], in_sems.at[i, 0])

    def base_copy(i):
        return pltpu.make_async_copy(base_hbm.at[0, rows_of(i)], b_buf.at[rows_of(i)], in_sems.at[i, 1])

    def out_copy(i):
        return pltpu.make_async_copy(o_buf.at[i], out_hbm.at[:, :, rows_of(i)], out_sems.at[i])

    keep_copy = pltpu.make_async_copy(keep_hbm, k_buf, k_sem)
    def fetch(i):
        delta_copy(i).start()
        base_copy(i).start()

    keep_copy.start()
    fetch(0)
    keep_copy.wait()
    spread_flags(k_buf, spread_ref, columns)
    for i in range(1, n):
        fetch(i)

    def chunk(i, carry):
        delta_copy(i).wait()
        base_copy(i).wait()
        for c in range(columns // LANES):
            cols = pl.ds(c * LANES, LANES)
            t = trimmed_tile(lambda k: d_buf[k, rows_of(i), cols], spread_ref, c, i * blocks)
            base = b_buf[rows_of(i), cols].astype(jnp.float32).reshape(blocks, 8, LANES)
            merged = (base + voted_update(t)).reshape(STEP, LANES).astype(jnp.bfloat16)
            turned = merged.T.reshape(4, LANES // 4, STEP)
            for j in range(4):
                o_buf[i, PLACE_OF[c * 4 + j]] = turned[j]
        out_copy(i).start()
        return carry

    lax.fori_loop(0, n, chunk, 0)
    for i in range(n):
        out_copy(i).wait()


def merge(base_weights, deltas, keep_turned):
    _, rows, columns = base_weights.shape
    n = rows // STEP
    slots = len(ORDER)
    return pl.pallas_call(
        merge_kernel,
        in_specs=[pl.BlockSpec(memory_space=pl.ANY)] * 3,
        out_specs=pl.BlockSpec(memory_space=pl.ANY),
        out_shape=jax.ShapeDtypeStruct((slots, columns // slots, rows), jnp.bfloat16),
        scratch_shapes=[
            pltpu.VMEM((3, rows, columns), jnp.bfloat16),
            pltpu.VMEM((rows, columns), jnp.bfloat16),
            pltpu.VMEM((n, slots, columns // slots, STEP), jnp.bfloat16),
            pltpu.VMEM(keep_turned.shape, jnp.int32),
            spread_scratch(rows, columns),
            pltpu.SemaphoreType.DMA((n, 2)),
            pltpu.SemaphoreType.DMA((n,)),
            pltpu.SemaphoreType.DMA,
        ],
        compiler_params=pltpu.CompilerParams(vmem_limit_bytes=VMEM_BYTES),
    )(keep_turned, base_weights, deltas)


def figures_kernel(keep_ref, delta_ref, merged_ref, sums_ref, largest_ref, spread_ref):
    step = pl.program_id(0)
    columns = delta_ref.shape[3]
    blocks = STEP // 8

    @pl.when(step == 0)
    def _():
        sums_ref[...] = jnp.zeros_like(sums_ref)
        largest_ref[...] = jnp.zeros_like(largest_ref)
        spread_flags(keep_ref, spread_ref, columns)

    largest = largest_ref[...]
    for c in range(columns // LANES):
        cols = pl.ds(c * LANES, LANES)
        t = trimmed_tile(lambda k: delta_ref[k, 0, :, cols], spread_ref, c, step * blocks)
        largest = jnp.maximum(largest, jnp.abs(voted_update(t)).max(axis=0))
    largest_ref[...] = largest
    total = sums_ref[...]
    for s in range(merged_ref.shape[0]):
        m = merged_ref[s].astype(jnp.float32)
        total = total + m.reshape(m.shape[0] // 8, 8, LANES).sum(axis=0)
    sums_ref[...] = total


def figures(keep_turned, deltas, merged):
    _, _, rows, columns = deltas.shape
    slots, height, _ = merged.shape
    return pl.pallas_call(
        figures_kernel,
        grid=(rows // STEP,),
        in_specs=[
            pl.BlockSpec(keep_turned.shape, lambda i: (0, 0, 0, 0)),
            pl.BlockSpec((3, 1, STEP, columns), lambda i: (0, 0, i, 0)),
            pl.BlockSpec((slots, height, STEP), lambda i: (0, 0, i)),
        ],
        out_specs=[pl.BlockSpec((8, LANES), lambda i: (0, 0))] * 2,
        out_shape=[jax.ShapeDtypeStruct((8, LANES), jnp.float32)] * 2,
        scratch_shapes=[spread_scratch(rows, columns)],
        compiler_params=pltpu.CompilerParams(vmem_limit_bytes=VMEM_BYTES),
    )(keep_turned, deltas, merged)


def totals_kernel(both_ref, total_ref, largest_ref):
    total_ref[0] = jnp.sum(both_ref[:, 0:1]) * (1.0 / math.sqrt(D * F))
    largest_ref[0] = jnp.max(both_ref[:, 1:2])


def totals(both):
    one = jax.ShapeDtypeStruct((1,), jnp.float32)
    return pl.pallas_call(
        totals_kernel,
        in_specs=[pl.BlockSpec(memory_space=pltpu.VMEM)],
        out_specs=[pl.BlockSpec(memory_space=pltpu.SMEM)] * 2,
        out_shape=[one, one],
    )(both)


def place_kernel(order_ref, place_ref, in_ref, out_ref, sems):
    def copy(s):
        return pltpu.make_async_copy(in_ref.at[place_ref[order_ref[s]]], out_ref.at[s], sems.at[s])

    for s in range(out_ref.shape[0]):
        copy(s).start()
    for s in range(out_ref.shape[0]):
        copy(s).wait()


def place(arranged, serve_order):
    n = arranged.shape[0]
    return pl.pallas_call(
        place_kernel,
        in_specs=[
            pl.BlockSpec(memory_space=pltpu.SMEM),
            pl.BlockSpec(memory_space=pltpu.SMEM),
            pl.BlockSpec(memory_space=pl.ANY),
        ],
        out_specs=pl.BlockSpec(memory_space=pl.ANY),
        out_shape=jax.ShapeDtypeStruct(arranged.shape, arranged.dtype),
        scratch_shapes=[pltpu.SemaphoreType.DMA((n,))],
        compiler_params=pltpu.CompilerParams(vmem_limit_bytes=4 * 2**20),
    )(serve_order, jnp.array(PLACE_OF, jnp.int32), arranged)


def on_device(base_weights, deltas, keep_flags, serve_order):
    keep_turned = jnp.swapaxes(keep_flags, 2, 3)
    merged = merge(base_weights, deltas, keep_turned)
    arranged = lax.all_to_all(
        merged, "expert", split_axis=0, concat_axis=0, tiled=True, axis_index_groups=[ORDER]
    )
    sums, largest = figures(keep_turned, deltas, merged)
    here = jnp.stack([jnp.sum(sums), jnp.max(largest)])
    both = lax.all_gather(here, "mp")
    total, largest = totals(both)
    serving = place(arranged, serve_order)
    return (serving, total, largest)


def solution(mesh):
    in_specs = (
        P("expert", "mp", None),
        P(None, "expert", "mp", None),
        P(None, "expert", "mp", None),
        P(),
    )
    out_specs = (P(None, "expert", "mp"), P("expert"), P("expert"))
    return jax.shard_map(
        on_device, mesh=mesh, in_specs=in_specs, out_specs=out_specs, check_vma=False
    )
```

```python
import math

import jax
import jax.numpy as jnp
from jax import lax
from jax.experimental import pallas as pl
from jax.experimental.pallas import tpu as pltpu
from jax.sharding import PartitionSpec as P

D = 7168
F = 1024
LANES = 128
STEP = 128
ORDER = [
    19, 28, 1, 17, 12, 22, 16, 30, 15, 6, 9, 31, 14, 25, 4, 26,
    2, 27, 13, 0, 5, 23, 11, 24, 18, 7, 3, 29, 20, 21, 8, 10,
]
PLACE_OF = [ORDER.index(e) for e in range(32)]
VMEM_BYTES = 60 * 2**20


def spread_flags(flags_ref, spread_ref, columns):
    for k in range(3):
        spread = spread_over_lanes(flags_ref[k, 0], columns)
        for c in range(columns // LANES):
            spread_ref[k, c, pl.ds(0, spread.shape[0])] = spread[:, c * LANES : (c + 1) * LANES]


def spread_scratch(rows, columns):
    return pltpu.VMEM((3, columns // LANES, rows // 8 + 8, LANES), jnp.float32)


def spread_over_lanes(flags, columns):
    lane_block = lax.broadcasted_iota(jnp.int32, (flags.shape[0], columns), 1) // LANES
    own_block = lax.broadcasted_iota(jnp.int32, (flags.shape[0], columns), 0)
    expand = (lane_block == own_block).astype(jnp.float32)
    return lax.dot_general(
        flags.astype(jnp.float32),
        expand,
        (((0,), (0,)), ((), ())),
        preferred_element_type=jnp.float32,
    )


def voted_update(t):
    s = t[0] + t[1] + t[2]
    sign = jnp.where(s > 0, 1.0, jnp.where(s < 0, -1.0, 0.0))
    a, b, c = (x * sign for x in t)
    low, high = jnp.minimum(a, b), jnp.maximum(a, b)
    most, least = jnp.maximum(high, c), jnp.minimum(low, c)
    middle = jnp.maximum(low, jnp.minimum(high, c))
    few = jnp.where(middle > 0, (most + middle) * 0.5, most) * sign
    return jnp.where(least > 0, s * (1.0 / 3.0), few)


def trimmed_tile(delta_at, spread_ref, column_block, first_block):
    out = []
    for k in range(3):
        d = delta_at(k).astype(jnp.float32)
        blocks = d.shape[0] // 8
        d = d.reshape(blocks, 8, LANES)
        kept = [spread_ref[k, column_block, pl.ds(first_block + r, 8, stride=0)] for r in range(blocks)]
        out.append(jnp.stack([d[r] * kept[r] for r in range(blocks)]))
    return out


def merge_kernel(
    keep_hbm, base_hbm, delta_hbm, out_hbm, d_buf, b_buf, o_buf, k_buf, spread_ref, in_sems, out_sems, k_sem
):
    rows_all, columns = b_buf.shape
    n = rows_all // STEP
    blocks = STEP // 8

    def rows_of(i):
        return pl.ds(pl.multiple_of(i * STEP, STEP), STEP)

    def delta_copy(i):
        return pltpu.make_async_copy(delta_hbm.at[:, 0, rows_of(i)], d_buf.at[:, rows_of(i)], in_sems.at[i, 0])

    def base_copy(i):
        return pltpu.make_async_copy(base_hbm.at[0, rows_of(i)], b_buf.at[rows_of(i)], in_sems.at[i, 1])

    def out_copy(i):
        return pltpu.make_async_copy(o_buf.at[i], out_hbm.at[:, :, rows_of(i)], out_sems.at[i])

    keep_copy = pltpu.make_async_copy(keep_hbm, k_buf, k_sem)
    def fetch(i):
        delta_copy(i).start()
        base_copy(i).start()

    keep_copy.start()
    fetch(0)
    keep_copy.wait()
    spread_flags(k_buf, spread_ref, columns)
    for i in range(1, n):
        fetch(i)

    def chunk(i, carry):
        delta_copy(i).wait()
        base_copy(i).wait()
        for c in range(columns // LANES):
            cols = pl.ds(c * LANES, LANES)
            t = trimmed_tile(lambda k: d_buf[k, rows_of(i), cols], spread_ref, c, i * blocks)
            base = b_buf[rows_of(i), cols].astype(jnp.float32).reshape(blocks, 8, LANES)
            merged = (base + voted_update(t)).reshape(STEP, LANES).astype(jnp.bfloat16)
            turned = merged.T.reshape(4, LANES // 4, STEP)
            for j in range(4):
                o_buf[i, PLACE_OF[c * 4 + j]] = turned[j]
        out_copy(i).start()
        return carry

    lax.fori_loop(0, n, chunk, 0)
    for i in range(n):
        out_copy(i).wait()


def merge(base_weights, deltas, keep_turned):
    _, rows, columns = base_weights.shape
    n = rows // STEP
    slots = len(ORDER)
    return pl.pallas_call(
        merge_kernel,
        in_specs=[pl.BlockSpec(memory_space=pl.ANY)] * 3,
        out_specs=pl.BlockSpec(memory_space=pl.ANY),
        out_shape=jax.ShapeDtypeStruct((slots, columns // slots, rows), jnp.bfloat16),
        scratch_shapes=[
            pltpu.VMEM((3, rows, columns), jnp.bfloat16),
            pltpu.VMEM((rows, columns), jnp.bfloat16),
            pltpu.VMEM((n, slots, columns // slots, STEP), jnp.bfloat16),
            pltpu.VMEM(keep_turned.shape, jnp.int32),
            spread_scratch(rows, columns),
            pltpu.SemaphoreType.DMA((n, 2)),
            pltpu.SemaphoreType.DMA((n,)),
            pltpu.SemaphoreType.DMA,
        ],
        compiler_params=pltpu.CompilerParams(vmem_limit_bytes=VMEM_BYTES),
    )(keep_turned, base_weights, deltas)


def figures_kernel(keep_ref, delta_ref, merged_ref, sums_ref, largest_ref, spread_ref):
    step = pl.program_id(0)
    columns = delta_ref.shape[3]
    blocks = STEP // 8

    @pl.when(step == 0)
    def _():
        sums_ref[...] = jnp.zeros_like(sums_ref)
        largest_ref[...] = jnp.zeros_like(largest_ref)
        spread_flags(keep_ref, spread_ref, columns)

    largest = largest_ref[...]
    for c in range(columns // LANES):
        cols = pl.ds(c * LANES, LANES)
        t = trimmed_tile(lambda k: delta_ref[k, 0, :, cols], spread_ref, c, step * blocks)
        largest = jnp.maximum(largest, jnp.abs(voted_update(t)).max(axis=0))
    largest_ref[...] = largest
    total = sums_ref[...]
    for s in range(merged_ref.shape[0]):
        m = merged_ref[s].astype(jnp.float32)
        total = total + m.reshape(m.shape[0] // 8, 8, LANES).sum(axis=0)
    sums_ref[...] = total


def figures(keep_turned, deltas, merged):
    _, _, rows, columns = deltas.shape
    slots, height, _ = merged.shape
    return pl.pallas_call(
        figures_kernel,
        grid=(rows // STEP,),
        in_specs=[
            pl.BlockSpec(keep_turned.shape, lambda i: (0, 0, 0, 0)),
            pl.BlockSpec((3, 1, STEP, columns), lambda i: (0, 0, i, 0)),
            pl.BlockSpec((slots, height, STEP), lambda i: (0, 0, i)),
        ],
        out_specs=[pl.BlockSpec((8, LANES), lambda i: (0, 0))] * 2,
        out_shape=[jax.ShapeDtypeStruct((8, LANES), jnp.float32)] * 2,
        scratch_shapes=[spread_scratch(rows, columns)],
        compiler_params=pltpu.CompilerParams(vmem_limit_bytes=VMEM_BYTES),
    )(keep_turned, deltas, merged)


def totals_kernel(both_ref, order_ref, place_ref, total_ref, largest_ref, source_ref):
    for s in range(source_ref.shape[0]):
        source_ref[s] = place_ref[order_ref[s]]
    total_ref[0] = jnp.sum(both_ref[:, 0:1]) * (1.0 / math.sqrt(D * F))
    largest_ref[0] = jnp.max(both_ref[:, 1:2])


def totals(both, serve_order):
    one = jax.ShapeDtypeStruct((1,), jnp.float32)
    return pl.pallas_call(
        totals_kernel,
        in_specs=[
            pl.BlockSpec(memory_space=pltpu.VMEM),
            pl.BlockSpec(memory_space=pltpu.SMEM),
            pl.BlockSpec(memory_space=pltpu.SMEM),
        ],
        out_specs=[pl.BlockSpec(memory_space=pltpu.SMEM)] * 3,
        out_shape=[one, one, pltpu.SMEM(serve_order.shape, jnp.int32)],
    )(both, serve_order, jnp.array(PLACE_OF, jnp.int32))


def place_kernel(source_ref, in_ref, out_ref, sems):
    def copy(s):
        return pltpu.make_async_copy(in_ref.at[source_ref[s]], out_ref.at[s], sems.at[s])

    for s in range(out_ref.shape[0]):
        copy(s).start()
    for s in range(out_ref.shape[0]):
        copy(s).wait()


def place(arranged, source):
    n = arranged.shape[0]
    return pl.pallas_call(
        place_kernel,
        in_specs=[
            pl.BlockSpec(memory_space=pltpu.SMEM),
            pl.BlockSpec(memory_space=pl.ANY),
        ],
        out_specs=pl.BlockSpec(memory_space=pl.ANY),
        out_shape=jax.ShapeDtypeStruct(arranged.shape, arranged.dtype),
        scratch_shapes=[pltpu.SemaphoreType.DMA((n,))],
        compiler_params=pltpu.CompilerParams(vmem_limit_bytes=4 * 2**20),
    )(source, arranged)


def on_device(base_weights, deltas, keep_flags, serve_order):
    keep_turned = jnp.swapaxes(keep_flags, 2, 3)
    merged = merge(base_weights, deltas, keep_turned)
    arranged = lax.all_to_all(
        merged, "expert", split_axis=0, concat_axis=0, tiled=True, axis_index_groups=[ORDER]
    )
    sums, largest = figures(keep_turned, deltas, merged)
    here = jnp.stack([jnp.sum(sums), jnp.max(largest)])
    both = lax.all_gather(here, "mp")
    total, largest, source = totals(both, serve_order)
    serving = place(arranged, source)
    return (serving, total, largest)


def solution(mesh):
    in_specs = (
        P("expert", "mp", None),
        P(None, "expert", "mp", None),
        P(None, "expert", "mp", None),
        P(),
    )
    out_specs = (P(None, "expert", "mp"), P("expert"), P("expert"))
    return jax.shard_map(
        on_device, mesh=mesh, in_specs=in_specs, out_specs=out_specs, check_vma=False
    )
```

```python
import math

import jax
import jax.numpy as jnp
from jax import lax
from jax.experimental import pallas as pl
from jax.experimental.pallas import tpu as pltpu
from jax.sharding import PartitionSpec as P

D = 7168
F = 1024
LANES = 128
STEP = 128
ORDER = [
    19, 28, 1, 17, 12, 22, 16, 31, 9, 6, 15, 30, 14, 25, 4, 26,
    2, 27, 13, 0, 5, 23, 11, 24, 18, 7, 3, 29, 20, 21, 8, 10,
]
PLACE_OF = [ORDER.index(e) for e in range(32)]
VMEM_BYTES = 60 * 2**20


def spread_flags(flags_ref, spread_ref, columns):
    for k in range(3):
        spread = spread_over_lanes(flags_ref[k, 0], columns)
        for c in range(columns // LANES):
            spread_ref[k, c, pl.ds(0, spread.shape[0])] = spread[:, c * LANES : (c + 1) * LANES]


def spread_scratch(rows, columns):
    return pltpu.VMEM((3, columns // LANES, rows // 8 + 8, LANES), jnp.float32)


def spread_over_lanes(flags, columns):
    lane_block = lax.broadcasted_iota(jnp.int32, (flags.shape[0], columns), 1) // LANES
    own_block = lax.broadcasted_iota(jnp.int32, (flags.shape[0], columns), 0)
    expand = (lane_block == own_block).astype(jnp.float32)
    return lax.dot_general(
        flags.astype(jnp.float32),
        expand,
        (((0,), (0,)), ((), ())),
        preferred_element_type=jnp.float32,
    )


def voted_update(t):
    s = t[0] + t[1] + t[2]
    sign = jnp.where(s > 0, 1.0, jnp.where(s < 0, -1.0, 0.0))
    a, b, c = (x * sign for x in t)
    low, high = jnp.minimum(a, b), jnp.maximum(a, b)
    most, least = jnp.maximum(high, c), jnp.minimum(low, c)
    middle = jnp.maximum(low, jnp.minimum(high, c))
    few = jnp.where(middle > 0, (most + middle) * 0.5, most) * sign
    return jnp.where(least > 0, s * (1.0 / 3.0), few)


def trimmed_tile(delta_at, spread_ref, column_block, first_block):
    out = []
    for k in range(3):
        d = delta_at(k).astype(jnp.float32)
        blocks = d.shape[0] // 8
        d = d.reshape(blocks, 8, LANES)
        kept = [spread_ref[k, column_block, pl.ds(first_block + r, 8, stride=0)] for r in range(blocks)]
        out.append(jnp.stack([d[r] * kept[r] for r in range(blocks)]))
    return out


def merge_kernel(
    keep_hbm, base_hbm, delta_hbm, out_hbm, d_buf, b_buf, o_buf, k_buf, spread_ref, in_sems, out_sems, k_sem
):
    rows_all, columns = b_buf.shape
    n = rows_all // STEP
    blocks = STEP // 8

    def rows_of(i):
        return pl.ds(pl.multiple_of(i * STEP, STEP), STEP)

    def delta_copy(i):
        return pltpu.make_async_copy(delta_hbm.at[:, 0, rows_of(i)], d_buf.at[:, rows_of(i)], in_sems.at[i, 0])

    def base_copy(i):
        return pltpu.make_async_copy(base_hbm.at[0, rows_of(i)], b_buf.at[rows_of(i)], in_sems.at[i, 1])

    def out_copy(i):
        return pltpu.make_async_copy(o_buf.at[i], out_hbm.at[:, :, rows_of(i)], out_sems.at[i])

    keep_copy = pltpu.make_async_copy(keep_hbm, k_buf, k_sem)
    def fetch(i):
        delta_copy(i).start()
        base_copy(i).start()

    keep_copy.start()
    fetch(0)
    keep_copy.wait()
    spread_flags(k_buf, spread_ref, columns)
    for i in range(1, n):
        fetch(i)

    def chunk(i, carry):
        delta_copy(i).wait()
        base_copy(i).wait()
        for c in range(columns // LANES):
            cols = pl.ds(c * LANES, LANES)
            t = trimmed_tile(lambda k: d_buf[k, rows_of(i), cols], spread_ref, c, i * blocks)
            base = b_buf[rows_of(i), cols].astype(jnp.float32).reshape(blocks, 8, LANES)
            merged = (base + voted_update(t)).reshape(STEP, LANES).astype(jnp.bfloat16)
            turned = merged.T.reshape(4, LANES // 4, STEP)
            for j in range(4):
                o_buf[i, PLACE_OF[c * 4 + j]] = turned[j]
        out_copy(i).start()
        return carry

    lax.fori_loop(0, n, chunk, 0)
    for i in range(n):
        out_copy(i).wait()


def merge(base_weights, deltas, keep_turned):
    _, rows, columns = base_weights.shape
    n = rows // STEP
    slots = len(ORDER)
    return pl.pallas_call(
        merge_kernel,
        in_specs=[pl.BlockSpec(memory_space=pl.ANY)] * 3,
        out_specs=pl.BlockSpec(memory_space=pl.ANY),
        out_shape=jax.ShapeDtypeStruct((slots, columns // slots, rows), jnp.bfloat16),
        scratch_shapes=[
            pltpu.VMEM((3, rows, columns), jnp.bfloat16),
            pltpu.VMEM((rows, columns), jnp.bfloat16),
            pltpu.VMEM((n, slots, columns // slots, STEP), jnp.bfloat16),
            pltpu.VMEM(keep_turned.shape, jnp.int32),
            spread_scratch(rows, columns),
            pltpu.SemaphoreType.DMA((n, 2)),
            pltpu.SemaphoreType.DMA((n,)),
            pltpu.SemaphoreType.DMA,
        ],
        compiler_params=pltpu.CompilerParams(vmem_limit_bytes=VMEM_BYTES),
    )(keep_turned, base_weights, deltas)


def figures_kernel(keep_ref, delta_ref, merged_ref, sums_ref, largest_ref, spread_ref):
    step = pl.program_id(0)
    columns = delta_ref.shape[3]
    blocks = STEP // 8

    @pl.when(step == 0)
    def _():
        sums_ref[...] = jnp.zeros_like(sums_ref)
        largest_ref[...] = jnp.zeros_like(largest_ref)
        spread_flags(keep_ref, spread_ref, columns)

    largest = largest_ref[...]
    for c in range(columns // LANES):
        cols = pl.ds(c * LANES, LANES)
        t = trimmed_tile(lambda k: delta_ref[k, 0, :, cols], spread_ref, c, step * blocks)
        largest = jnp.maximum(largest, jnp.abs(voted_update(t)).max(axis=0))
    largest_ref[...] = largest
    total = sums_ref[...]
    for s in range(merged_ref.shape[0]):
        m = merged_ref[s].astype(jnp.float32)
        total = total + m.reshape(m.shape[0] // 8, 8, LANES).sum(axis=0)
    sums_ref[...] = total


def figures(keep_turned, deltas, merged):
    _, _, rows, columns = deltas.shape
    slots, height, _ = merged.shape
    return pl.pallas_call(
        figures_kernel,
        grid=(rows // STEP,),
        in_specs=[
            pl.BlockSpec(keep_turned.shape, lambda i: (0, 0, 0, 0)),
            pl.BlockSpec((3, 1, STEP, columns), lambda i: (0, 0, i, 0)),
            pl.BlockSpec((slots, height, STEP), lambda i: (0, 0, i)),
        ],
        out_specs=[pl.BlockSpec((8, LANES), lambda i: (0, 0))] * 2,
        out_shape=[jax.ShapeDtypeStruct((8, LANES), jnp.float32)] * 2,
        scratch_shapes=[spread_scratch(rows, columns)],
        compiler_params=pltpu.CompilerParams(vmem_limit_bytes=VMEM_BYTES),
    )(keep_turned, deltas, merged)


def totals_kernel(both_ref, order_ref, place_ref, total_ref, largest_ref, source_ref):
    for s in range(source_ref.shape[0]):
        source_ref[s] = place_ref[order_ref[s]]
    total_ref[0] = jnp.sum(both_ref[:, 0:1]) * (1.0 / math.sqrt(D * F))
    largest_ref[0] = jnp.max(both_ref[:, 1:2])


def totals(both, serve_order):
    one = jax.ShapeDtypeStruct((1,), jnp.float32)
    return pl.pallas_call(
        totals_kernel,
        in_specs=[
            pl.BlockSpec(memory_space=pltpu.VMEM),
            pl.BlockSpec(memory_space=pltpu.SMEM),
            pl.BlockSpec(memory_space=pltpu.SMEM),
        ],
        out_specs=[pl.BlockSpec(memory_space=pltpu.SMEM)] * 3,
        out_shape=[one, one, pltpu.SMEM(serve_order.shape, jnp.int32)],
    )(both, serve_order, jnp.array(PLACE_OF, jnp.int32))


def place_kernel(source_ref, in_ref, out_ref, sems):
    def copy(s):
        return pltpu.make_async_copy(in_ref.at[source_ref[s]], out_ref.at[s], sems.at[s])

    for s in range(out_ref.shape[0]):
        copy(s).start()
    for s in range(out_ref.shape[0]):
        copy(s).wait()


def place(arranged, source):
    n = arranged.shape[0]
    return pl.pallas_call(
        place_kernel,
        in_specs=[
            pl.BlockSpec(memory_space=pltpu.SMEM),
            pl.BlockSpec(memory_space=pl.ANY),
        ],
        out_specs=pl.BlockSpec(memory_space=pl.ANY),
        out_shape=jax.ShapeDtypeStruct(arranged.shape, arranged.dtype),
        scratch_shapes=[pltpu.SemaphoreType.DMA((n,))],
        compiler_params=pltpu.CompilerParams(vmem_limit_bytes=4 * 2**20),
    )(source, arranged)


def on_device(base_weights, deltas, keep_flags, serve_order):
    keep_turned = jnp.swapaxes(keep_flags, 2, 3)
    merged = merge(base_weights, deltas, keep_turned)
    arranged = lax.all_to_all(
        merged, "expert", split_axis=0, concat_axis=0, tiled=True, axis_index_groups=[ORDER]
    )
    sums, largest = figures(keep_turned, deltas, merged)
    here = jnp.stack([jnp.sum(sums), jnp.max(largest)])
    both = lax.all_gather(here, "mp")
    total, largest, source = totals(both, serve_order)
    serving = place(arranged, source)
    return (serving, total, largest)


def solution(mesh):
    in_specs = (
        P("expert", "mp", None),
        P(None, "expert", "mp", None),
        P(None, "expert", "mp", None),
        P(),
    )
    out_specs = (P(None, "expert", "mp"), P("expert"), P("expert"))
    return jax.shard_map(
        on_device, mesh=mesh, in_specs=in_specs, out_specs=out_specs, check_vma=False
    )
```

```python
import math

import jax
import jax.numpy as jnp
from jax import lax
from jax.experimental import pallas as pl
from jax.experimental.pallas import tpu as pltpu
from jax.sharding import PartitionSpec as P

D = 7168
F = 1024
LANES = 128
STEP = 128
ORDER = [
    19, 28, 1, 17, 12, 22, 16, 31, 9, 6, 15, 30, 14, 25, 4, 26,
    2, 27, 13, 0, 5, 23, 11, 24, 18, 7, 3, 29, 20, 21, 8, 10,
]
PLACE_OF = [ORDER.index(e) for e in range(32)]
VMEM_BYTES = 60 * 2**20


def spread_flags(flags_ref, spread_ref, columns):
    for k in range(3):
        spread = spread_over_lanes(flags_ref[k, 0], columns)
        for c in range(columns // LANES):
            spread_ref[k, c, pl.ds(0, spread.shape[0])] = spread[:, c * LANES : (c + 1) * LANES]


def spread_scratch(rows, columns):
    return pltpu.VMEM((3, columns // LANES, rows // 8 + 8, LANES), jnp.float32)


def spread_over_lanes(flags, columns):
    lane_block = lax.broadcasted_iota(jnp.int32, (flags.shape[0], columns), 1) // LANES
    own_block = lax.broadcasted_iota(jnp.int32, (flags.shape[0], columns), 0)
    expand = (lane_block == own_block).astype(jnp.float32)
    return lax.dot_general(
        flags.astype(jnp.float32),
        expand,
        (((0,), (0,)), ((), ())),
        preferred_element_type=jnp.float32,
    )


def voted_update(t):
    t = [x.reshape(x.shape[0] * 8, LANES) for x in t]
    s = t[0] + t[1] + t[2]
    direction = s.astype(jnp.bfloat16)
    zero, one = jnp.bfloat16(0), jnp.bfloat16(1)
    sign = jnp.where(direction > zero, one, jnp.where(direction < zero, -one, zero))
    a, b, c = (x.astype(jnp.bfloat16) * sign for x in t)
    low, high = jnp.minimum(a, b), jnp.maximum(a, b)
    most, least = jnp.maximum(high, c), jnp.minimum(low, c)
    middle = jnp.maximum(low, jnp.minimum(high, c))
    second = jnp.where(middle > zero, middle, most)
    few = ((most * sign).astype(jnp.float32) + (second * sign).astype(jnp.float32)) * 0.5
    update = jnp.where(least.astype(jnp.float32) > 0, s * (1.0 / 3.0), few)
    return update.reshape(update.shape[0] // 8, 8, LANES)


def trimmed_tile(delta_at, spread_ref, column_block, first_block):
    out = []
    for k in range(3):
        d = delta_at(k).astype(jnp.float32)
        blocks = d.shape[0] // 8
        d = d.reshape(blocks, 8, LANES)
        kept = [spread_ref[k, column_block, pl.ds(first_block + r, 8, stride=0)] for r in range(blocks)]
        out.append(jnp.stack([d[r] * kept[r] for r in range(blocks)]))
    return out


def merge_kernel(
    keep_hbm, base_hbm, delta_hbm, out_hbm, d_buf, b_buf, o_buf, k_buf, spread_ref, in_sems, out_sems, k_sem
):
    rows_all, columns = b_buf.shape
    n = rows_all // STEP
    blocks = STEP // 8

    def rows_of(i):
        return pl.ds(pl.multiple_of(i * STEP, STEP), STEP)

    def delta_copy(i):
        return pltpu.make_async_copy(delta_hbm.at[:, 0, rows_of(i)], d_buf.at[:, rows_of(i)], in_sems.at[i, 0])

    def base_copy(i):
        return pltpu.make_async_copy(base_hbm.at[0, rows_of(i)], b_buf.at[rows_of(i)], in_sems.at[i, 1])

    def out_copy(i):
        return pltpu.make_async_copy(o_buf.at[i], out_hbm.at[:, :, rows_of(i)], out_sems.at[i])

    keep_copy = pltpu.make_async_copy(keep_hbm, k_buf, k_sem)
    def fetch(i):
        delta_copy(i).start()
        base_copy(i).start()

    keep_copy.start()
    fetch(0)
    keep_copy.wait()
    spread_flags(k_buf, spread_ref, columns)
    for i in range(1, n):
        fetch(i)

    def chunk(i, carry):
        delta_copy(i).wait()
        base_copy(i).wait()
        for c in range(columns // LANES):
            cols = pl.ds(c * LANES, LANES)
            t = trimmed_tile(lambda k: d_buf[k, rows_of(i), cols], spread_ref, c, i * blocks)
            base = b_buf[rows_of(i), cols].astype(jnp.float32).reshape(blocks, 8, LANES)
            merged = (base + voted_update(t)).reshape(STEP, LANES).astype(jnp.bfloat16)
            turned = merged.T.reshape(4, LANES // 4, STEP)
            for j in range(4):
                o_buf[i, PLACE_OF[c * 4 + j]] = turned[j]
        out_copy(i).start()
        return carry

    lax.fori_loop(0, n, chunk, 0)
    for i in range(n):
        out_copy(i).wait()


def merge(base_weights, deltas, keep_turned):
    _, rows, columns = base_weights.shape
    n = rows // STEP
    slots = len(ORDER)
    return pl.pallas_call(
        merge_kernel,
        in_specs=[pl.BlockSpec(memory_space=pl.ANY)] * 3,
        out_specs=pl.BlockSpec(memory_space=pl.ANY),
        out_shape=jax.ShapeDtypeStruct((slots, columns // slots, rows), jnp.bfloat16),
        scratch_shapes=[
            pltpu.VMEM((3, rows, columns), jnp.bfloat16),
            pltpu.VMEM((rows, columns), jnp.bfloat16),
            pltpu.VMEM((n, slots, columns // slots, STEP), jnp.bfloat16),
            pltpu.VMEM(keep_turned.shape, jnp.int32),
            spread_scratch(rows, columns),
            pltpu.SemaphoreType.DMA((n, 2)),
            pltpu.SemaphoreType.DMA((n,)),
            pltpu.SemaphoreType.DMA,
        ],
        compiler_params=pltpu.CompilerParams(vmem_limit_bytes=VMEM_BYTES),
    )(keep_turned, base_weights, deltas)


def figures_kernel(keep_ref, delta_ref, merged_ref, sums_ref, largest_ref, spread_ref):
    step = pl.program_id(0)
    columns = delta_ref.shape[3]
    blocks = STEP // 8

    @pl.when(step == 0)
    def _():
        sums_ref[...] = jnp.zeros_like(sums_ref)
        largest_ref[...] = jnp.zeros_like(largest_ref)
        spread_flags(keep_ref, spread_ref, columns)

    largest = largest_ref[...]
    for c in range(columns // LANES):
        cols = pl.ds(c * LANES, LANES)
        t = trimmed_tile(lambda k: delta_ref[k, 0, :, cols], spread_ref, c, step * blocks)
        largest = jnp.maximum(largest, jnp.abs(voted_update(t)).max(axis=0))
    largest_ref[...] = largest
    total = sums_ref[...]
    for s in range(merged_ref.shape[0]):
        m = merged_ref[s].astype(jnp.float32)
        total = total + m.reshape(m.shape[0] // 8, 8, LANES).sum(axis=0)
    sums_ref[...] = total


def figures(keep_turned, deltas, merged):
    _, _, rows, columns = deltas.shape
    slots, height, _ = merged.shape
    return pl.pallas_call(
        figures_kernel,
        grid=(rows // STEP,),
        in_specs=[
            pl.BlockSpec(keep_turned.shape, lambda i: (0, 0, 0, 0)),
            pl.BlockSpec((3, 1, STEP, columns), lambda i: (0, 0, i, 0)),
            pl.BlockSpec((slots, height, STEP), lambda i: (0, 0, i)),
        ],
        out_specs=[pl.BlockSpec((8, LANES), lambda i: (0, 0))] * 2,
        out_shape=[jax.ShapeDtypeStruct((8, LANES), jnp.float32)] * 2,
        scratch_shapes=[spread_scratch(rows, columns)],
        compiler_params=pltpu.CompilerParams(vmem_limit_bytes=VMEM_BYTES),
    )(keep_turned, deltas, merged)


def totals_kernel(both_ref, order_ref, place_ref, total_ref, largest_ref, source_ref):
    for s in range(source_ref.shape[0]):
        source_ref[s] = place_ref[order_ref[s]]
    total_ref[0] = jnp.sum(both_ref[:, 0:1]) * (1.0 / math.sqrt(D * F))
    largest_ref[0] = jnp.max(both_ref[:, 1:2])


def totals(both, serve_order):
    one = jax.ShapeDtypeStruct((1,), jnp.float32)
    return pl.pallas_call(
        totals_kernel,
        in_specs=[
            pl.BlockSpec(memory_space=pltpu.VMEM),
            pl.BlockSpec(memory_space=pltpu.SMEM),
            pl.BlockSpec(memory_space=pltpu.SMEM),
        ],
        out_specs=[pl.BlockSpec(memory_space=pltpu.SMEM)] * 3,
        out_shape=[one, one, pltpu.SMEM(serve_order.shape, jnp.int32)],
    )(both, serve_order, jnp.array(PLACE_OF, jnp.int32))


def place_kernel(source_ref, in_ref, out_ref, sems):
    def copy(s):
        return pltpu.make_async_copy(in_ref.at[source_ref[s]], out_ref.at[s], sems.at[s])

    for s in range(out_ref.shape[0]):
        copy(s).start()
    for s in range(out_ref.shape[0]):
        copy(s).wait()


def place(arranged, source):
    n = arranged.shape[0]
    return pl.pallas_call(
        place_kernel,
        in_specs=[
            pl.BlockSpec(memory_space=pltpu.SMEM),
            pl.BlockSpec(memory_space=pl.ANY),
        ],
        out_specs=pl.BlockSpec(memory_space=pl.ANY),
        out_shape=jax.ShapeDtypeStruct(arranged.shape, arranged.dtype),
        scratch_shapes=[pltpu.SemaphoreType.DMA((n,))],
        compiler_params=pltpu.CompilerParams(vmem_limit_bytes=4 * 2**20),
    )(source, arranged)


def on_device(base_weights, deltas, keep_flags, serve_order):
    keep_turned = jnp.swapaxes(keep_flags, 2, 3)
    merged = merge(base_weights, deltas, keep_turned)
    arranged = lax.all_to_all(
        merged, "expert", split_axis=0, concat_axis=0, tiled=True, axis_index_groups=[ORDER]
    )
    sums, largest = figures(keep_turned, deltas, merged)
    here = jnp.stack([jnp.sum(sums), jnp.max(largest)])
    both = lax.all_gather(here, "mp")
    total, largest, source = totals(both, serve_order)
    serving = place(arranged, source)
    return (serving, total, largest)


def solution(mesh):
    in_specs = (
        P("expert", "mp", None),
        P(None, "expert", "mp", None),
        P(None, "expert", "mp", None),
        P(),
    )
    out_specs = (P(None, "expert", "mp"), P("expert"), P("expert"))
    return jax.shard_map(
        on_device, mesh=mesh, in_specs=in_specs, out_specs=out_specs, check_vma=False
    )
```
